32 devices in a mesh: grp: 2 (over x), dev: 16 (over z, y, core).
Axes of the slice: x: 2, y: 2, z: 4, core: 2. Of those that a mesh axis runs over, the one named last changes fastest.
Arguments:
- stream: bfloat16 [512, 4096], P('grp'), may hold values from -6 to 6
- row_length: int32 [4], P('grp'), may hold values from 1 to 128, as said below
- row_start: int32 [4], P('grp'), may hold values from 0 to 2047
- attn_gain: float32 [4096], replicated, may hold values from 0.1 to 1.9
- w_query: bfloat16 [4096, 4096], P('grp', 'dev'), as said below
- w_key: bfloat16 [4096, 1024], P('grp', 'dev'), may hold values from -0.09375 to 0.09375
- w_value: bfloat16 [4096, 1024], P('grp', 'dev'), may hold values from -0.09375 to 0.09375
- w_out: bfloat16 [4096, 4096], P('grp', 'dev'), may hold values from -0.09375 to 0.09375
- ffn_gain: float32 [4096], replicated, may hold values from 0.1 to 1.9
- w_gate: bfloat16 [4096, 14336], P('grp', 'dev'), may hold values from -0.09375 to 0.09375
- w_up: bfloat16 [4096, 14336], P('grp', 'dev'), may hold values from -0.09375 to 0.09375
- w_down: bfloat16 [4096, 14336], P('grp', 'dev'), may hold values from -0.046875 to 0.046875
Outputs:
- key_cache: bfloat16 [512, 1024], P('grp', 'dev')
- value_cache: bfloat16 [512, 1024], P('grp', 'dev')
- next_stream: bfloat16 [512, 4096], P('grp', 'dev')
The draws below stay inside these ranges and needn't reach their ends.
Inputs may be any that keep to these rules, and one draw needn't show every extreme that they name: `row_length`: in every draw some row holds all 128 slots cached and some row only one. `row_start`: position of each row's first slot. `w_query`: query projection with independent entries.
All inputs are finite; a program needn't handle non-finite values.
Results may differ from the reference program's by a relative error of at most 0.011.
The reference program's roundings to bfloat16 on the way (of `normed`, `probs`, `mixed`, `attended`, `normed2` and `hidden`) count: a program that leaves them out, or rounds other values in their place, can miss the bound.
Values may be sent and summed in bfloat16 or wider, within the bound.
A program may use at most 128 MiB of HBM per device.

```python
import math
import jax
import jax.numpy as jnp
from jax import lax

D = 4096
FF = 14336
HEADS = 32
KV_HEADS = 8
HEAD_DIM = 128
ROW_LEN = 128
KVD = 1024
ALL_ROWS = 4
TOKENS = 512


def draw_w_query(key, part):
    key = jax.random.fold_in(key, 11)
    factor = 1.0
    entries = jax.random.normal(key, (D, D), jnp.float32)
    return (entries * (factor / math.sqrt(D))).astype(jnp.bfloat16)


def draw_row_length(key, part):
    key = jax.random.fold_in(key, 23)
    first_key, second_key = jax.random.split(key)
    lengths = jax.random.randint(first_key, (ALL_ROWS,), 1, ROW_LEN + 1)
    order = jax.random.permutation(second_key, ALL_ROWS)
    lengths = lengths.at[order[0]].set(ROW_LEN)
    lengths = lengths.at[order[1]].set(1)
    return lengths.astype(jnp.int32)


def place_ends(result, own_key, least, top_value):
    extent = result.shape
    index_at = [jax.random.randint(jax.random.fold_in(own_key, axis), (), 0, extent[axis]) for axis in range(len(extent))]
    result = result.at[tuple(index_at)].set(least)
    longest = extent.index(max(extent))
    index_at[longest] = (index_at[longest] + 1) % extent[longest]
    return result.at[tuple(index_at)].set(top_value)


def level_of(key, dims, pieces, smallest, high):
    def one(axis_at, shards_of):
        steps = jax.random.uniform(jax.random.fold_in(jax.random.fold_in(key, 6), axis_at), (shards_of,), jnp.float32, smallest / len(pieces), high / len(pieces))
        return jnp.repeat(jnp.exp(steps), dims[axis_at] // shards_of).reshape((-1,) + (1,) * (len(dims) - axis_at - 1))

    loudness = one(*pieces[0])
    for cut in pieces[1:]:
        loudness = loudness * one(*cut)
    return loudness


def gaussian(rng, extent, deviation, most, pieces=(), kind=jnp.bfloat16):
    values = deviation * jax.random.normal(rng, extent, jnp.float32)
    if pieces:
        values = values * level_of(rng, extent, pieces, -0.22, 0.18)
    return jnp.clip(values, -most, most).astype(kind)


def setup_inputs(seed: int = 0) -> dict:
    arg_keys = jax.random.split(jax.random.key(seed), 13)
    stream = gaussian(arg_keys[0], (TOKENS, D), 1.0, 6.0, ((0, 2),))
    row_length = draw_row_length(jax.random.fold_in(arg_keys[12], 71), 0)
    row_start = place_ends(jax.random.randint(arg_keys[2], (ALL_ROWS,), 0, 2048), jax.random.fold_in(arg_keys[2], 1), 0, 2047).astype(jnp.int32)
    attn_gain = jnp.clip(1.0 + 0.18 * jax.random.normal(arg_keys[3], (D,), jnp.float32), 0.1, 1.9)
    w_query = draw_w_query(jax.random.fold_in(arg_keys[12], 71), 0)
    w_key = gaussian(arg_keys[5], (D, KVD), D ** -0.5, 0.09375, ((0, 2), (1, 16)))
    w_value = gaussian(arg_keys[6], (D, KVD), D ** -0.5, 0.09375, ((0, 2), (1, 16)))
    w_out = gaussian(arg_keys[7], (D, D), D ** -0.5, 0.09375, ((0, 2), (1, 16)))
    ffn_gain = jnp.clip(1.0 + 0.18 * jax.random.normal(arg_keys[8], (D,), jnp.float32), 0.1, 1.9)
    w_gate = gaussian(arg_keys[9], (D, FF), D ** -0.5, 0.09375, ((0, 2), (1, 16)))
    w_up = gaussian(arg_keys[10], (D, FF), D ** -0.5, 0.09375, ((0, 2), (1, 16)))
    w_down = gaussian(arg_keys[11], (D, FF), FF ** -0.5, 0.046875, ((0, 2), (1, 16)))
    return {"stream": stream, "row_length": row_length, "row_start": row_start, "attn_gain": attn_gain, "w_query": w_query, "w_key": w_key, "w_value": w_value, "w_out": w_out, "ffn_gain": ffn_gain, "w_gate": w_gate, "w_up": w_up, "w_down": w_down}


rope_base = 500000.0

def norm_rows(values, gain):
    return values * lax.rsqrt(lax.optimization_barrier(jnp.mean(values * values, axis=-1, keepdims=True)) + 1e-05) * gain

def rotate(values, positions, first):
    cols = first + jnp.arange(values.shape[1], dtype=jnp.int32)
    pair = (cols % HEAD_DIM // 2).astype(jnp.float32)
    freq = jnp.exp(-(2.0 * pair / HEAD_DIM) * math.log(rope_base))
    angle = positions.astype(jnp.float32)[:, None] * freq[None, :]
    lead = values.reshape(values.shape[0], -1, 2)
    partner = jnp.stack([-lead[..., 1], lead[..., 0]], axis=-1).reshape(values.shape)
    return values * jnp.cos(angle) + partner * jnp.sin(angle)

def attend_row(packed):
    queries, keys, values, length = packed
    group = HEADS // KV_HEADS
    count = queries.shape[0]
    qh = queries.astype(jnp.float32).reshape(count, KV_HEADS, group, HEAD_DIM)
    kh = keys.astype(jnp.float32).reshape(-1, KV_HEADS, HEAD_DIM)
    vh = values.astype(jnp.float32).reshape(-1, KV_HEADS, HEAD_DIM)
    scores = jnp.einsum('qkgd,jkd->kgqj', qh, kh) / math.sqrt(HEAD_DIM)
    query_pos = jnp.arange(count, dtype=jnp.int32)
    key_pos = jnp.arange(keys.shape[0], dtype=jnp.int32)
    allowed = (key_pos[None, :] <= query_pos[:, None]) & (key_pos[None, :] < length)
    scores = jnp.where(allowed, scores, -jnp.inf)
    top = lax.optimization_barrier(jnp.max(scores, axis=-1, keepdims=True))
    expo = jnp.exp(scores - top)
    probs = (expo / lax.optimization_barrier(jnp.sum(expo, axis=-1, keepdims=True))).astype(jnp.bfloat16)
    mixed = jnp.einsum('kgqj,jkd->qkgd', probs.astype(jnp.float32), vh)
    return mixed.astype(jnp.bfloat16).reshape(count, -1)

def reference(stream, row_length, row_start, attn_gain, w_query, w_key, w_value, w_out, ffn_gain, w_gate, w_up, w_down):
    positions = (row_start[:, None] + jnp.arange(ROW_LEN, dtype=jnp.int32)[None, :]).reshape(-1)
    normed = norm_rows(stream.astype(jnp.float32), attn_gain).astype(jnp.bfloat16)
    queries = rotate(jnp.dot(normed, w_query, preferred_element_type=jnp.float32), positions, 0).astype(jnp.bfloat16)
    keys = rotate(jnp.dot(normed, w_key, preferred_element_type=jnp.float32), positions, 0).astype(jnp.bfloat16)
    values = jnp.dot(normed, w_value, preferred_element_type=jnp.float32).astype(jnp.bfloat16)
    mixed = lax.map(attend_row, (queries.reshape(ALL_ROWS, ROW_LEN, D), keys.reshape(ALL_ROWS, ROW_LEN, KVD), values.reshape(ALL_ROWS, ROW_LEN, KVD), row_length))
    mixed = mixed.reshape(TOKENS, D)
    attended = (stream.astype(jnp.float32) + jnp.dot(mixed, w_out, preferred_element_type=jnp.float32)).astype(jnp.bfloat16)
    normed2 = norm_rows(attended.astype(jnp.float32), ffn_gain).astype(jnp.bfloat16)
    gate = jnp.dot(normed2, w_gate, preferred_element_type=jnp.float32)
    up = jnp.dot(normed2, w_up, preferred_element_type=jnp.float32)
    hidden = (jax.nn.silu(gate) * up).astype(jnp.bfloat16)
    down = lax.dot_general(hidden, w_down, (((1,), (1,)), ((), ())), preferred_element_type=jnp.float32)
    next_stream = (attended.astype(jnp.float32) + down).astype(jnp.bfloat16)
    return (keys, values, next_stream)
```

```python
import math

import jax
import jax.numpy as jnp
from jax import lax
from jax.sharding import PartitionSpec as P

HEADS = 32
KV_HEADS = 8
HEAD_DIM = 128
ROW_LEN = 128


rope_base = 500000.0


def norm_rows(values, gain):
    return values * lax.rsqrt(jnp.mean(values * values, axis=-1, keepdims=True) + 1e-05) * gain


def rotate(values, positions, first):
    cols = first + jnp.arange(values.shape[1], dtype=jnp.int32)
    pair = (cols % HEAD_DIM // 2).astype(jnp.float32)
    freq = jnp.exp(-(2.0 * pair / HEAD_DIM) * math.log(rope_base))
    angle = positions.astype(jnp.float32)[:, None] * freq[None, :]
    lead = values.reshape(values.shape[0], -1, 2)
    partner = jnp.stack([-lead[..., 1], lead[..., 0]], axis=-1).reshape(values.shape)
    return values * jnp.cos(angle) + partner * jnp.sin(angle)


def attend(queries, keys, values, offset, length):
    group = HEADS // KV_HEADS
    count = queries.shape[0]
    qh = queries.reshape(count, KV_HEADS, group, HEAD_DIM)
    kh = keys.reshape(-1, KV_HEADS, HEAD_DIM)
    vh = values.reshape(-1, KV_HEADS, HEAD_DIM)
    scores = jnp.einsum("qkgd,jkd->kgqj", qh, kh, preferred_element_type=jnp.float32) / math.sqrt(
        HEAD_DIM
    )
    query_pos = offset + jnp.arange(count, dtype=jnp.int32)
    key_pos = jnp.arange(keys.shape[0], dtype=jnp.int32)
    allowed = (key_pos[None, :] <= query_pos[:, None]) & (key_pos[None, :] < length)
    scores = jnp.where(allowed, scores, -jnp.inf)
    top = jnp.max(scores, axis=-1, keepdims=True)
    expo = jnp.exp(scores - top)
    probs = (expo / jnp.sum(expo, axis=-1, keepdims=True)).astype(jnp.bfloat16)
    mixed = jnp.einsum("kgqj,jkd->qkgd", probs, vh, preferred_element_type=jnp.float32)
    return mixed.astype(jnp.bfloat16).reshape(count, -1)


def gathered_weights(
    stream,
    row_length,
    row_start,
    attn_gain,
    w_query,
    w_key,
    w_value,
    w_out,
    ffn_gain,
    w_gate,
    w_up,
    w_down,
):
    member = lax.axis_index("dev")
    members = lax.axis_size("dev")
    w_query, w_key, w_value, w_out, w_gate, w_up, w_down = (
        lax.all_gather(w_query, "grp", axis=0, tiled=True),
        lax.all_gather(w_key, "grp", axis=0, tiled=True),
        lax.all_gather(w_value, "grp", axis=0, tiled=True),
        lax.all_gather(w_out, "grp", axis=0, tiled=True),
        lax.all_gather(w_gate, "grp", axis=0, tiled=True),
        lax.all_gather(w_up, "grp", axis=0, tiled=True),
        lax.all_gather(w_down, "grp", axis=0, tiled=True),
    )
    slots = stream.shape[0]
    query_cols = w_query.shape[1]
    kv_cols = w_key.shape[1]
    positions = (row_start[:, None] + jnp.arange(ROW_LEN, dtype=jnp.int32)[None, :]).reshape(-1)
    normed = norm_rows(stream.astype(jnp.float32), attn_gain).astype(jnp.bfloat16)
    queries = rotate(
        jnp.dot(normed, w_query, preferred_element_type=jnp.float32), positions, member * query_cols
    ).astype(jnp.bfloat16)
    keys = rotate(
        jnp.dot(normed, w_key, preferred_element_type=jnp.float32), positions, member * kv_cols
    ).astype(jnp.bfloat16)
    values = jnp.dot(normed, w_value, preferred_element_type=jnp.float32).astype(jnp.bfloat16)
    share = slots // members
    first = member * share
    all_queries, all_keys, all_values = (
        lax.all_gather(queries, "dev", axis=1, tiled=True),
        lax.all_gather(keys, "dev", axis=1, tiled=True),
        lax.all_gather(values, "dev", axis=1, tiled=True),
    )
    own_queries = lax.dynamic_slice_in_dim(all_queries, first, share, 0)
    row_index = first // ROW_LEN
    row_keys = lax.dynamic_slice_in_dim(all_keys, row_index * ROW_LEN, ROW_LEN, 0)
    row_values = lax.dynamic_slice_in_dim(all_values, row_index * ROW_LEN, ROW_LEN, 0)
    length = lax.dynamic_index_in_dim(row_length, row_index, 0, keepdims=False)
    mixed = attend(own_queries, row_keys, row_values, first - row_index * ROW_LEN, length)
    projected = jnp.dot(
        lax.all_gather(mixed, "dev", axis=0, tiled=True), w_out, preferred_element_type=jnp.float32
    )
    own_stream = lax.dynamic_slice_in_dim(stream, member * query_cols, query_cols, 1)
    attended = (own_stream.astype(jnp.float32) + projected).astype(jnp.bfloat16)
    full_rows = lax.all_gather(attended, "dev", axis=1, tiled=True)
    normed2 = norm_rows(full_rows.astype(jnp.float32), ffn_gain).astype(jnp.bfloat16)
    gate = jnp.dot(normed2, w_gate, preferred_element_type=jnp.float32)
    up = jnp.dot(normed2, w_up, preferred_element_type=jnp.float32)
    hidden = (jax.nn.silu(gate) * up).astype(jnp.bfloat16)
    partial_down = lax.dot_general(
        hidden, w_down, (((1,), (1,)), ((), ())), preferred_element_type=jnp.float32
    )
    summed = lax.psum_scatter(partial_down, "dev", scatter_dimension=1, tiled=True)
    next_stream = (attended.astype(jnp.float32) + summed).astype(jnp.bfloat16)
    return (keys, values, next_stream)


def across(values):
    return lax.ppermute(values, "grp", [(0, 1), (1, 0)])


def beside(values, bit):
    members = lax.axis_size("dev")
    return lax.ppermute(values, "dev", [(i, i ^ bit) for i in range(members)])


def corner(values):
    members = lax.axis_size("dev")
    top = members // 2
    pairs = []
    for grp in range(2):
        for dev in range(members):
            if dev // top != grp:
                pairs.append((grp * members + dev, (1 - grp) * members + (dev ^ top)))
    return lax.ppermute(values, ("grp", "dev"), pairs)


def pick(values, index, axis):
    return lax.dynamic_index_in_dim(values, index, axis, keepdims=False)


def after(values, *earlier):
    return lax.optimization_barrier((values,) + earlier)[0]


def turn(values, cos, sin):
    even = jnp.arange(values.shape[1], dtype=jnp.int32) % 2 == 0
    partner = jnp.where(even[None, :], -jnp.roll(values, -1, axis=1), jnp.roll(values, 1, axis=1))
    return values * cos + partner * sin


def halve(values, axis, bit, mine):
    return pick(values, mine, axis) + beside(pick(values, 1 - mine, axis), bit)


def dot(a, b):
    return jnp.dot(a, b, preferred_element_type=jnp.float32)


def dot_t(a, b):
    return lax.dot_general(a, b, (((1,), (1,)), ((), ())), preferred_element_type=jnp.float32)


def moved_rows(
    stream,
    row_length,
    row_start,
    attn_gain,
    w_query,
    w_key,
    w_value,
    w_out,
    ffn_gain,
    w_gate,
    w_up,
    w_down,
):
    grp = lax.axis_index("grp")
    member = lax.axis_index("dev")
    members = lax.axis_size("dev")
    core, y, z_lo = member % 2, member // 2 % 2, member // 4 % 2
    slots, width = stream.shape
    half = width // 2
    part = slots // 2
    block = w_query.shape[1]
    kv_cols = w_key.shape[1]
    rows = slots // ROW_LEN
    blocks = half // block

    normed = norm_rows(stream.astype(jnp.float32), attn_gain).astype(jnp.bfloat16)
    got = across(lax.dynamic_slice(normed, (core * part, (1 - grp) * half), (part, half)))
    sib = beside(got, 1)
    w_all = jnp.concatenate([w_query, w_key, w_value], axis=1)
    back_got = across(dot(got, w_all))
    back_sib = across(dot(sib, w_all))
    own = dot(lax.dynamic_slice_in_dim(normed, grp * half, half, 1), w_all)
    lo = jnp.where(core == 0, back_got, back_sib)
    hi = jnp.where(core == 0, back_sib, back_got)
    total = own + jnp.concatenate([lo, hi], axis=0)

    positions = (row_start[:, None] + jnp.arange(ROW_LEN, dtype=jnp.int32)[None, :]).reshape(-1)
    pair = (jnp.arange(HEAD_DIM, dtype=jnp.int32) // 2).astype(jnp.float32)
    freq = jnp.exp(-(2.0 * pair / HEAD_DIM) * math.log(rope_base))
    angle = positions.astype(jnp.float32)[:, None] * freq[None, :]
    cos, sin = jnp.cos(angle), jnp.sin(angle)
    heads = block // HEAD_DIM
    queries = turn(
        total[:, :block], jnp.tile(cos, (1, heads)), jnp.tile(sin, (1, heads))
    ).astype(jnp.bfloat16)
    key_first = core * kv_cols
    keys = turn(
        total[:, block : block + kv_cols],
        lax.dynamic_slice_in_dim(cos, key_first, kv_cols, 1),
        lax.dynamic_slice_in_dim(sin, key_first, kv_cols, 1),
    ).astype(jnp.bfloat16)
    values = total[:, block + kv_cols :].astype(jnp.bfloat16)

    mine = jnp.stack([keys, values])
    theirs = beside(mine, 1)
    both = jnp.where(
        core == 0,
        jnp.concatenate([mine, theirs], axis=2),
        jnp.concatenate([theirs, mine], axis=2),
    )
    qh = queries.reshape(rows, ROW_LEN, heads, HEAD_DIM)
    kh = both[0].reshape(rows, ROW_LEN, HEAD_DIM)
    vh = both[1].reshape(rows, ROW_LEN, HEAD_DIM)
    scores = jnp.einsum("rqhd,rjd->rhqj", qh, kh, preferred_element_type=jnp.float32) / math.sqrt(
        HEAD_DIM
    )
    at = jnp.arange(ROW_LEN, dtype=jnp.int32)
    allowed = (at[None, None, :] <= at[None, :, None]) & (
        at[None, None, :] < row_length[:, None, None]
    )
    scores = jnp.where(allowed[:, None], scores, -jnp.inf)
    top = jnp.max(scores, axis=-1, keepdims=True)
    expo = jnp.exp(scores - top)
    probs = (expo / jnp.sum(expo, axis=-1, keepdims=True)).astype(jnp.bfloat16)
    mixed = jnp.einsum("rhqj,rjd->rqhd", probs, vh, preferred_element_type=jnp.float32)
    mixed = mixed.astype(jnp.bfloat16).reshape(slots, block)

    w_out_far = across(after(w_out, back_got, back_sib))
    all_mixed = lax.all_gather(mixed, "dev", axis=0, tiled=False)

    def by_blocks(blocked, weight):
        return lax.dot_general(
            blocked,
            weight.reshape(blocks, block, -1),
            (((0, 2), (0, 1)), ((), ())),
            preferred_element_type=jnp.float32,
        )

    projected = by_blocks(
        lax.dynamic_slice_in_dim(all_mixed, grp * blocks, blocks, 0), w_out
    ) + by_blocks(lax.dynamic_slice_in_dim(all_mixed, (1 - grp) * blocks, blocks, 0), w_out_far)
    own_stream = lax.dynamic_slice_in_dim(stream, member * block, block, 1)
    attended = (own_stream.astype(jnp.float32) + projected).astype(jnp.bfloat16)
    all_attended = lax.all_gather(attended, "dev", axis=0, tiled=False)
    far_attended = corner(attended)

    wide = all_attended.astype(jnp.float32)
    mean = jnp.mean(jnp.mean(wide * wide, axis=2, keepdims=True), axis=0, keepdims=True)
    normed2 = (
        wide * lax.rsqrt(mean + 1e-05) * ffn_gain.reshape(members, 1, block)
    ).astype(jnp.bfloat16)
    got2 = across(
        lax.dynamic_slice(normed2, ((1 - grp) * blocks, core * part, 0), (blocks, part, block))
    )
    sib2 = beside(got2, 1)
    gate_got = across(by_blocks(got2, w_gate))
    up_got = across(by_blocks(got2, w_up))
    gate_sib = across(by_blocks(sib2, w_gate))
    up_sib = across(by_blocks(sib2, w_up))
    near = lax.dynamic_slice_in_dim(normed2, grp * blocks, blocks, 0)
    near_got = lax.dynamic_slice_in_dim(near, core * part, part, 1)
    near_sib = lax.dynamic_slice_in_dim(near, (1 - core) * part, part, 1)

    def gated(rows_near, gate_far, up_far):
        gate = by_blocks(rows_near, w_gate) + gate_far
        up = by_blocks(rows_near, w_up) + up_far
        return (jax.nn.silu(gate) * up).astype(jnp.bfloat16)

    hidden_got = gated(near_got, gate_got, up_got)
    hidden_sib = gated(near_sib, gate_sib, up_sib)
    far_got = across(hidden_got)
    far_sib = across(hidden_sib)

    def placed(a, b):
        lower = jnp.where(core == 0, a, b)
        upper = jnp.where(core == 0, b, a)
        return jnp.concatenate([lower, upper], axis=0)

    near_hidden = placed(hidden_got, hidden_sib)
    far_hidden = placed(far_got, far_sib)
    w_pairs = w_down.reshape(blocks // 2, 2, block, -1)
    w_send = pick(w_pairs, 1 - core, 1)
    w_keep = pick(w_pairs, core, 1)

    def down(rows_in, weight):
        out = dot_t(rows_in, weight.reshape(-1, weight.shape[-1]))
        return out.reshape(slots, blocks // 2, block)

    def stage(rows_in):
        return down(rows_in, w_keep) + beside(down(rows_in, w_send), 1)

    near_sum, far_sum = stage(near_hidden), stage(far_hidden)

    def folded(sums):
        return jnp.moveaxis(sums, 1, 0).reshape(2, 2, slots, block)

    is_near = member // (members // 2) == grp
    near_sum, far_sum = folded(near_sum), folded(far_sum)
    keep_all = jnp.stack([near_sum, far_sum])
    side = jnp.where(is_near, 0, 1)
    one, two = keep_all[:, :, :, :part], keep_all[:, :, :, part:]
    one = halve(one, 2, 2, y)
    two = halve(two, 1, 4, z_lo)
    one = halve(one, 1, 4, z_lo)
    two = halve(two, 0, 8, side)
    one = halve(one, 0, 8, side)
    two = halve(two, 0, 2, y)
    summed = jnp.concatenate([one, two], axis=0)
    base = jnp.where(is_near, attended, far_attended)
    done = (base.astype(jnp.float32) + summed).astype(jnp.bfloat16)
    next_stream = jnp.where(is_near, done, corner(done))
    return (keys, values, next_stream)


def solution(mesh):
    exact = dict(mesh.shape) == {"grp": 2, "dev": 16}
    on_device = moved_rows if exact else gathered_weights
    placed = (
        P("grp", None),
        P("grp"),
        P("grp"),
        P(),
        P("grp", "dev"),
        P("grp", "dev"),
        P("grp", "dev"),
        P("grp", "dev"),
        P(),
        P("grp", "dev"),
        P("grp", "dev"),
        P("grp", "dev"),
    )
    return jax.shard_map(
        on_device,
        mesh=mesh,
        in_specs=placed,
        out_specs=(P("grp", "dev"), P("grp", "dev"), P("grp", "dev")),
        check_vma=False,
    )
```

```python
import math

import jax
import jax.numpy as jnp
from jax import lax
from jax.sharding import PartitionSpec as P

HEADS = 32
KV_HEADS = 8
HEAD_DIM = 128
ROW_LEN = 128


rope_base = 500000.0
wire = jnp.float32


def norm_rows(values, gain):
    return values * lax.rsqrt(jnp.mean(values * values, axis=-1, keepdims=True) + 1e-05) * gain


def rotate(values, positions, first):
    cols = first + jnp.arange(values.shape[1], dtype=jnp.int32)
    pair = (cols % HEAD_DIM // 2).astype(jnp.float32)
    freq = jnp.exp(-(2.0 * pair / HEAD_DIM) * math.log(rope_base))
    angle = positions.astype(jnp.float32)[:, None] * freq[None, :]
    lead = values.reshape(values.shape[0], -1, 2)
    partner = jnp.stack([-lead[..., 1], lead[..., 0]], axis=-1).reshape(values.shape)
    return values * jnp.cos(angle) + partner * jnp.sin(angle)


def attend(queries, keys, values, offset, length):
    group = HEADS // KV_HEADS
    count = queries.shape[0]
    qh = queries.reshape(count, KV_HEADS, group, HEAD_DIM)
    kh = keys.reshape(-1, KV_HEADS, HEAD_DIM)
    vh = values.reshape(-1, KV_HEADS, HEAD_DIM)
    scores = jnp.einsum("qkgd,jkd->kgqj", qh, kh, preferred_element_type=jnp.float32) / math.sqrt(
        HEAD_DIM
    )
    query_pos = offset + jnp.arange(count, dtype=jnp.int32)
    key_pos = jnp.arange(keys.shape[0], dtype=jnp.int32)
    allowed = (key_pos[None, :] <= query_pos[:, None]) & (key_pos[None, :] < length)
    scores = jnp.where(allowed, scores, -jnp.inf)
    top = jnp.max(scores, axis=-1, keepdims=True)
    expo = jnp.exp(scores - top)
    probs = (expo / jnp.sum(expo, axis=-1, keepdims=True)).astype(jnp.bfloat16)
    mixed = jnp.einsum("kgqj,jkd->qkgd", probs, vh, preferred_element_type=jnp.float32)
    return mixed.astype(jnp.bfloat16).reshape(count, -1)


def gathered_weights(
    stream,
    row_length,
    row_start,
    attn_gain,
    w_query,
    w_key,
    w_value,
    w_out,
    ffn_gain,
    w_gate,
    w_up,
    w_down,
):
    member = lax.axis_index("dev")
    members = lax.axis_size("dev")
    w_query, w_key, w_value, w_out, w_gate, w_up, w_down = (
        lax.all_gather(w_query, "grp", axis=0, tiled=True),
        lax.all_gather(w_key, "grp", axis=0, tiled=True),
        lax.all_gather(w_value, "grp", axis=0, tiled=True),
        lax.all_gather(w_out, "grp", axis=0, tiled=True),
        lax.all_gather(w_gate, "grp", axis=0, tiled=True),
        lax.all_gather(w_up, "grp", axis=0, tiled=True),
        lax.all_gather(w_down, "grp", axis=0, tiled=True),
    )
    slots = stream.shape[0]
    query_cols = w_query.shape[1]
    kv_cols = w_key.shape[1]
    positions = (row_start[:, None] + jnp.arange(ROW_LEN, dtype=jnp.int32)[None, :]).reshape(-1)
    normed = norm_rows(stream.astype(jnp.float32), attn_gain).astype(jnp.bfloat16)
    queries = rotate(
        jnp.dot(normed, w_query, preferred_element_type=jnp.float32), positions, member * query_cols
    ).astype(jnp.bfloat16)
    keys = rotate(
        jnp.dot(normed, w_key, preferred_element_type=jnp.float32), positions, member * kv_cols
    ).astype(jnp.bfloat16)
    values = jnp.dot(normed, w_value, preferred_element_type=jnp.float32).astype(jnp.bfloat16)
    share = slots // members
    first = member * share
    all_queries, all_keys, all_values = (
        lax.all_gather(queries, "dev", axis=1, tiled=True),
        lax.all_gather(keys, "dev", axis=1, tiled=True),
        lax.all_gather(values, "dev", axis=1, tiled=True),
    )
    own_queries = lax.dynamic_slice_in_dim(all_queries, first, share, 0)
    row_index = first // ROW_LEN
    row_keys = lax.dynamic_slice_in_dim(all_keys, row_index * ROW_LEN, ROW_LEN, 0)
    row_values = lax.dynamic_slice_in_dim(all_values, row_index * ROW_LEN, ROW_LEN, 0)
    length = lax.dynamic_index_in_dim(row_length, row_index, 0, keepdims=False)
    mixed = attend(own_queries, row_keys, row_values, first - row_index * ROW_LEN, length)
    projected = jnp.dot(
        lax.all_gather(mixed, "dev", axis=0, tiled=True), w_out, preferred_element_type=jnp.float32
    )
    own_stream = lax.dynamic_slice_in_dim(stream, member * query_cols, query_cols, 1)
    attended = (own_stream.astype(jnp.float32) + projected).astype(jnp.bfloat16)
    full_rows = lax.all_gather(attended, "dev", axis=1, tiled=True)
    normed2 = norm_rows(full_rows.astype(jnp.float32), ffn_gain).astype(jnp.bfloat16)
    gate = jnp.dot(normed2, w_gate, preferred_element_type=jnp.float32)
    up = jnp.dot(normed2, w_up, preferred_element_type=jnp.float32)
    hidden = (jax.nn.silu(gate) * up).astype(jnp.bfloat16)
    partial_down = lax.dot_general(
        hidden, w_down, (((1,), (1,)), ((), ())), preferred_element_type=jnp.float32
    )
    summed = lax.psum_scatter(partial_down, "dev", scatter_dimension=1, tiled=True)
    next_stream = (attended.astype(jnp.float32) + summed).astype(jnp.bfloat16)
    return (keys, values, next_stream)


def across(values):
    return lax.ppermute(values, "grp", [(0, 1), (1, 0)])


def beside(values, bit):
    members = lax.axis_size("dev")
    return lax.ppermute(values, "dev", [(i, i ^ bit) for i in range(members)])


def corner(values):
    members = lax.axis_size("dev")
    top = members // 2
    pairs = []
    for grp in range(2):
        for dev in range(members):
            if dev // top != grp:
                pairs.append((grp * members + dev, (1 - grp) * members + (dev ^ top)))
    return lax.ppermute(values, ("grp", "dev"), pairs)


def pick(values, index, axis):
    return lax.dynamic_index_in_dim(values, index, axis, keepdims=False)


def after(values, *earlier):
    return lax.optimization_barrier((values,) + earlier)[0]


def turn(values, cos, sin):
    even = jnp.arange(values.shape[1], dtype=jnp.int32) % 2 == 0
    partner = jnp.where(even[None, :], -jnp.roll(values, -1, axis=1), jnp.roll(values, 1, axis=1))
    return values * cos + partner * sin


def halve(values, axis, bit, mine):
    away = pick(values, 1 - mine, axis).astype(wire)
    return pick(values, mine, axis) + beside(away, bit).astype(jnp.float32)


def grow(values, axis, bit, mine):
    theirs = beside(values, bit)
    return jnp.where(
        mine == 0,
        jnp.concatenate([values, theirs], axis=axis),
        jnp.concatenate([theirs, values], axis=axis),
    )


def across_sum(values):
    return across(values.astype(wire)).astype(jnp.float32)


def dot(a, b):
    return jnp.dot(a, b, preferred_element_type=jnp.float32)


def dot_t(a, b):
    return lax.dot_general(a, b, (((1,), (1,)), ((), ())), preferred_element_type=jnp.float32)


def moved_rows(
    stream,
    row_length,
    row_start,
    attn_gain,
    w_query,
    w_key,
    w_value,
    w_out,
    ffn_gain,
    w_gate,
    w_up,
    w_down,
):
    grp = lax.axis_index("grp")
    member = lax.axis_index("dev")
    members = lax.axis_size("dev")
    core, y, z_lo = member % 2, member // 2 % 2, member // 4 % 2
    slots, width = stream.shape
    half = width // 2
    part = slots // 2
    block = w_query.shape[1]
    kv_cols = w_key.shape[1]
    rows = slots // ROW_LEN
    blocks = half // block

    got = across(lax.dynamic_slice(stream, (core * part, (1 - grp) * half), (part, half)))
    sib = beside(got, 1)
    wide = stream.astype(jnp.float32)
    scale = lax.rsqrt(jnp.mean(wide * wide, axis=-1, keepdims=True) + 1e-05)
    far_scale = across(scale)
    half_gain = lax.dynamic_slice_in_dim(attn_gain, grp * half, half, 0)

    def scaled(rows_in, factor):
        return (rows_in.astype(jnp.float32) * factor * half_gain).astype(jnp.bfloat16)

    got = scaled(got, lax.dynamic_slice_in_dim(far_scale, core * part, part, 0))
    sib = scaled(sib, lax.dynamic_slice_in_dim(far_scale, (1 - core) * part, part, 0))
    near = scaled(lax.dynamic_slice_in_dim(stream, grp * half, half, 1), scale)
    w_all = jnp.concatenate([w_query, w_key, w_value], axis=1)
    back_got = across(dot(got, w_all))
    back_sib = across(dot(sib, w_all))
    own = dot(near, w_all)
    lo = jnp.where(core == 0, back_got, back_sib)
    hi = jnp.where(core == 0, back_sib, back_got)
    total = own + jnp.concatenate([lo, hi], axis=0)

    positions = (row_start[:, None] + jnp.arange(ROW_LEN, dtype=jnp.int32)[None, :]).reshape(-1)
    pair = (jnp.arange(HEAD_DIM, dtype=jnp.int32) // 2).astype(jnp.float32)
    freq = jnp.exp(-(2.0 * pair / HEAD_DIM) * math.log(rope_base))
    angle = positions.astype(jnp.float32)[:, None] * freq[None, :]
    cos, sin = jnp.cos(angle), jnp.sin(angle)
    heads = block // HEAD_DIM
    queries = turn(
        total[:, :block], jnp.tile(cos, (1, heads)), jnp.tile(sin, (1, heads))
    ).astype(jnp.bfloat16)
    key_first = core * kv_cols
    keys = turn(
        total[:, block : block + kv_cols],
        lax.dynamic_slice_in_dim(cos, key_first, kv_cols, 1),
        lax.dynamic_slice_in_dim(sin, key_first, kv_cols, 1),
    ).astype(jnp.bfloat16)
    values = total[:, block + kv_cols :].astype(jnp.bfloat16)

    mine = jnp.stack([keys, values])
    theirs = beside(mine, 1)
    both = jnp.where(
        core == 0,
        jnp.concatenate([mine, theirs], axis=2),
        jnp.concatenate([theirs, mine], axis=2),
    )
    qh = queries.reshape(rows, ROW_LEN, heads, HEAD_DIM)
    kh = both[0].reshape(rows, ROW_LEN, HEAD_DIM)
    vh = both[1].reshape(rows, ROW_LEN, HEAD_DIM)
    scores = jnp.einsum("rqhd,rjd->rhqj", qh, kh, preferred_element_type=jnp.float32) / math.sqrt(
        HEAD_DIM
    )
    at = jnp.arange(ROW_LEN, dtype=jnp.int32)
    allowed = (at[None, None, :] <= at[None, :, None]) & (
        at[None, None, :] < row_length[:, None, None]
    )
    scores = jnp.where(allowed[:, None], scores, -jnp.inf)
    top = jnp.max(scores, axis=-1, keepdims=True)
    expo = jnp.exp(scores - top)
    probs = (expo / jnp.sum(expo, axis=-1, keepdims=True)).astype(jnp.bfloat16)
    mixed = jnp.einsum("rhqj,rjd->rqhd", probs, vh, preferred_element_type=jnp.float32)
    mixed = mixed.astype(jnp.bfloat16).reshape(slots, block)

    z_hi = member // 8
    place = {8: (0, z_hi), 4: (1, z_lo), 2: (2, y), 1: (3, core)}
    orders = ((8, 4, 2), (2, 8, 4))

    def spread(rows_in, bits):
        for bit in bits:
            rows_in = grow(rows_in, place[bit][0], bit, place[bit][1])
        return rows_in

    def by_blocks(blocked, weight):
        return lax.dot_general(
            blocked.reshape(blocks, part, block),
            weight.reshape(blocks, block, -1),
            (((0, 2), (0, 1)), ((), ())),
            preferred_element_type=jnp.float32,
        )

    w_out_far = across(after(w_out, back_got, back_sib))
    own_stream = lax.dynamic_slice_in_dim(stream, member * block, block, 1)
    gains = ffn_gain.reshape(2, blocks, 1, block)
    half_gain = pick(gains, grp, 0)
    attended, near_rows, far_rows = [], [], []
    for piece, order in enumerate(orders):
        span = slice(piece * part, (piece + 1) * part)
        all_mixed = spread(mixed[span].reshape(1, 1, 1, 1, part, block), order + (1,))
        projected = by_blocks(pick(all_mixed, grp, 0), w_out) + by_blocks(
            pick(all_mixed, 1 - grp, 0), w_out_far
        )
        own = (own_stream[span].astype(jnp.float32) + projected).astype(jnp.bfloat16)
        attended.append(own)
        some = spread(own.reshape(1, 1, 1, 1, part, block), order)
        got = across(pick(some, 1 - grp, 0))
        full = spread(some, (1,)).reshape(2, blocks, part, block)
        wide = full.astype(jnp.float32)
        mean = jnp.mean(jnp.mean(wide * wide, axis=3, keepdims=True), axis=(0, 1))
        scale = lax.rsqrt(mean + 1e-05)
        far_scale = across(scale)
        far = grow(got, 2, 1, core).reshape(blocks, part, block)
        near = pick(full, grp, 0).astype(jnp.float32)
        near_rows.append((near * scale * half_gain).astype(jnp.bfloat16))
        far_rows.append((far.astype(jnp.float32) * far_scale * half_gain).astype(jnp.bfloat16))
    far_attended = corner(jnp.concatenate(attended, axis=0))

    gate_far, up_far = [], []
    for far in far_rows:
        gate_far.append(across_sum(by_blocks(far, w_gate)))
        up_far.append(across_sum(by_blocks(far, w_up)))
    w_pairs = w_down.reshape(blocks // 2, 2, block, -1)
    w_send = pick(w_pairs, 1 - core, 1)
    w_keep = pick(w_pairs, core, 1)

    def down(rows_in, weight):
        return jnp.stack([dot_t(rows_in, weight[i]) for i in range(blocks // 2)])

    def summed_pairs(rows_in, piece):
        sums = down(rows_in, w_keep) + beside(down(rows_in, w_send), 1)
        sums = sums.reshape(2, 2, part, block)
        if piece == 0:
            return halve(halve(sums, 1, 2, y), 0, 4, z_lo)
        return halve(halve(sums, 0, 4, z_lo), 0, 2, y)

    is_near = z_hi == grp
    side = jnp.where(is_near, 0, 1)
    near_sums, far_sums = [], []
    for piece in range(2):
        gate = by_blocks(near_rows[piece], w_gate) + gate_far[piece]
        up = by_blocks(near_rows[piece], w_up) + up_far[piece]
        hidden = (jax.nn.silu(gate) * up).astype(jnp.bfloat16)
        far_hidden = across(hidden)
        near_sums.append(summed_pairs(hidden, piece))
        far_sums.append(summed_pairs(far_hidden, piece))
    done = []
    for piece in range(2):
        span = slice(piece * part, (piece + 1) * part)
        total = halve(jnp.stack([near_sums[piece], far_sums[piece]]), 0, 8, side)
        base = jnp.where(is_near, attended[piece], far_attended[span])
        ours = (base.astype(jnp.float32) + total).astype(jnp.bfloat16)
        done.append(jnp.where(is_near, ours, corner(ours)))
    return (keys, values, jnp.concatenate(done, axis=0))


def solution(mesh):
    exact = dict(mesh.shape) == {"grp": 2, "dev": 16}
    on_device = moved_rows if exact else gathered_weights
    placed = (
        P("grp", None),
        P("grp"),
        P("grp"),
        P(),
        P("grp", "dev"),
        P("grp", "dev"),
        P("grp", "dev"),
        P("grp", "dev"),
        P(),
        P("grp", "dev"),
        P("grp", "dev"),
        P("grp", "dev"),
    )
    return jax.shard_map(
        on_device,
        mesh=mesh,
        in_specs=placed,
        out_specs=(P("grp", "dev"), P("grp", "dev"), P("grp", "dev")),
        check_vma=False,
    )
```

```python
import functools
import math

import jax
import jax.numpy as jnp
from jax import lax
from jax.experimental import pallas as pl
from jax.experimental.pallas import tpu as pltpu
from jax.sharding import PartitionSpec as P

HEADS = 32
KV_HEADS = 8
HEAD_DIM = 128
ROW_LEN = 128


rope_base = 500000.0
wire = jnp.float32


def norm_rows(values, gain):
    return values * lax.rsqrt(jnp.mean(values * values, axis=-1, keepdims=True) + 1e-05) * gain


def rotate(values, positions, first):
    cols = first + jnp.arange(values.shape[1], dtype=jnp.int32)
    pair = (cols % HEAD_DIM // 2).astype(jnp.float32)
    freq = jnp.exp(-(2.0 * pair / HEAD_DIM) * math.log(rope_base))
    angle = positions.astype(jnp.float32)[:, None] * freq[None, :]
    lead = values.reshape(values.shape[0], -1, 2)
    partner = jnp.stack([-lead[..., 1], lead[..., 0]], axis=-1).reshape(values.shape)
    return values * jnp.cos(angle) + partner * jnp.sin(angle)


def attend(queries, keys, values, offset, length):
    group = HEADS // KV_HEADS
    count = queries.shape[0]
    qh = queries.reshape(count, KV_HEADS, group, HEAD_DIM)
    kh = keys.reshape(-1, KV_HEADS, HEAD_DIM)
    vh = values.reshape(-1, KV_HEADS, HEAD_DIM)
    scores = jnp.einsum("qkgd,jkd->kgqj", qh, kh, preferred_element_type=jnp.float32) / math.sqrt(
        HEAD_DIM
    )
    query_pos = offset + jnp.arange(count, dtype=jnp.int32)
    key_pos = jnp.arange(keys.shape[0], dtype=jnp.int32)
    allowed = (key_pos[None, :] <= query_pos[:, None]) & (key_pos[None, :] < length)
    scores = jnp.where(allowed, scores, -jnp.inf)
    top = jnp.max(scores, axis=-1, keepdims=True)
    expo = jnp.exp(scores - top)
    probs = (expo / jnp.sum(expo, axis=-1, keepdims=True)).astype(jnp.bfloat16)
    mixed = jnp.einsum("kgqj,jkd->qkgd", probs, vh, preferred_element_type=jnp.float32)
    return mixed.astype(jnp.bfloat16).reshape(count, -1)


def gathered_weights(
    stream,
    row_length,
    row_start,
    attn_gain,
    w_query,
    w_key,
    w_value,
    w_out,
    ffn_gain,
    w_gate,
    w_up,
    w_down,
):
    member = lax.axis_index("dev")
    members = lax.axis_size("dev")
    w_query, w_key, w_value, w_out, w_gate, w_up, w_down = (
        lax.all_gather(w_query, "grp", axis=0, tiled=True),
        lax.all_gather(w_key, "grp", axis=0, tiled=True),
        lax.all_gather(w_value, "grp", axis=0, tiled=True),
        lax.all_gather(w_out, "grp", axis=0, tiled=True),
        lax.all_gather(w_gate, "grp", axis=0, tiled=True),
        lax.all_gather(w_up, "grp", axis=0, tiled=True),
        lax.all_gather(w_down, "grp", axis=0, tiled=True),
    )
    slots = stream.shape[0]
    query_cols = w_query.shape[1]
    kv_cols = w_key.shape[1]
    positions = (row_start[:, None] + jnp.arange(ROW_LEN, dtype=jnp.int32)[None, :]).reshape(-1)
    normed = norm_rows(stream.astype(jnp.float32), attn_gain).astype(jnp.bfloat16)
    queries = rotate(
        jnp.dot(normed, w_query, preferred_element_type=jnp.float32), positions, member * query_cols
    ).astype(jnp.bfloat16)
    keys = rotate(
        jnp.dot(normed, w_key, preferred_element_type=jnp.float32), positions, member * kv_cols
    ).astype(jnp.bfloat16)
    values = jnp.dot(normed, w_value, preferred_element_type=jnp.float32).astype(jnp.bfloat16)
    share = slots // members
    first = member * share
    all_queries, all_keys, all_values = (
        lax.all_gather(queries, "dev", axis=1, tiled=True),
        lax.all_gather(keys, "dev", axis=1, tiled=True),
        lax.all_gather(values, "dev", axis=1, tiled=True),
    )
    own_queries = lax.dynamic_slice_in_dim(all_queries, first, share, 0)
    row_index = first // ROW_LEN
    row_keys = lax.dynamic_slice_in_dim(all_keys, row_index * ROW_LEN, ROW_LEN, 0)
    row_values = lax.dynamic_slice_in_dim(all_values, row_index * ROW_LEN, ROW_LEN, 0)
    length = lax.dynamic_index_in_dim(row_length, row_index, 0, keepdims=False)
    mixed = attend(own_queries, row_keys, row_values, first - row_index * ROW_LEN, length)
    projected = jnp.dot(
        lax.all_gather(mixed, "dev", axis=0, tiled=True), w_out, preferred_element_type=jnp.float32
    )
    own_stream = lax.dynamic_slice_in_dim(stream, member * query_cols, query_cols, 1)
    attended = (own_stream.astype(jnp.float32) + projected).astype(jnp.bfloat16)
    full_rows = lax.all_gather(attended, "dev", axis=1, tiled=True)
    normed2 = norm_rows(full_rows.astype(jnp.float32), ffn_gain).astype(jnp.bfloat16)
    gate = jnp.dot(normed2, w_gate, preferred_element_type=jnp.float32)
    up = jnp.dot(normed2, w_up, preferred_element_type=jnp.float32)
    hidden = (jax.nn.silu(gate) * up).astype(jnp.bfloat16)
    partial_down = lax.dot_general(
        hidden, w_down, (((1,), (1,)), ((), ())), preferred_element_type=jnp.float32
    )
    summed = lax.psum_scatter(partial_down, "dev", scatter_dimension=1, tiled=True)
    next_stream = (attended.astype(jnp.float32) + summed).astype(jnp.bfloat16)
    return (keys, values, next_stream)


def across(values):
    return lax.ppermute(values, "grp", [(0, 1), (1, 0)])


def beside(values, bit):
    members = lax.axis_size("dev")
    return lax.ppermute(values, "dev", [(i, i ^ bit) for i in range(members)])


def corner(values):
    members = lax.axis_size("dev")
    top = members // 2
    pairs = []
    for grp in range(2):
        for dev in range(members):
            if dev // top != grp:
                pairs.append((grp * members + dev, (1 - grp) * members + (dev ^ top)))
    return lax.ppermute(values, ("grp", "dev"), pairs)


def pick(values, index, axis):
    return lax.dynamic_index_in_dim(values, index, axis, keepdims=False)


def after(values, *earlier):
    return lax.optimization_barrier((values,) + earlier)[0]


def turn(values, cos, sin):
    even = jnp.arange(values.shape[1], dtype=jnp.int32) % 2 == 0
    partner = jnp.where(even[None, :], -jnp.roll(values, -1, axis=1), jnp.roll(values, 1, axis=1))
    return values * cos + partner * sin


def halve(values, axis, bit, mine):
    away = pick(values, 1 - mine, axis).astype(wire)
    return pick(values, mine, axis) + beside(away, bit).astype(jnp.float32)


def across_sum(values):
    return across(values.astype(wire)).astype(jnp.float32)


def dot(a, b):
    return jnp.dot(a, b, preferred_element_type=jnp.float32)


def dot_t(a, b):
    return lax.dot_general(a, b, (((1,), (1,)), ((), ())), preferred_element_type=jnp.float32)


link_orders = ((8, 4, 2, 1), (2, 8, 4, 1))


def flipped(index, bits):
    for bit in (8, 4, 2, 1):
        if bits & bit:
            index = index + bit * (1 - 2 * (index // bit % 2))
    return index


def subsets(bits):
    found = [0]
    for bit in bits:
        found = found + [have | bit for have in found]
    return found


def spread_kernel(both_groups, src_ref, out_ref, *rest):
    if both_groups:
        far_ref, send_sem, recv_sem, far_send, far_recv = rest
    else:
        send_sem, recv_sem = rest
    grp, me = lax.axis_index("grp"), lax.axis_index("dev")
    core = me % 2
    barrier = pltpu.get_barrier_semaphore()
    targets = [{"dev": flipped(me, bit)} for bit in (8, 4, 2, 1)]
    if both_groups:
        targets.append({"grp": 1 - grp})
    for target in targets:
        pl.semaphore_signal(
            barrier, inc=1, device_id=target, device_id_type=pl.DeviceIdType.MESH
        )
    pl.semaphore_wait(barrier, len(targets))

    pieces = len(link_orders)
    copies, far_copies, near_copies = {}, {}, {}

    def copy_to(source, target, sent, arrived):
        copy = pltpu.make_async_remote_copy(
            src_ref=source,
            dst_ref=target[0],
            send_sem=sent,
            recv_sem=arrived,
            device_id=target[1],
            device_id_type=pl.DeviceIdType.MESH,
        )
        copy.start()
        return copy

    def forward(piece, have):
        order = link_orders[piece]
        later = 1 + max([order.index(bit) for bit in order if have & bit], default=-1)
        block = out_ref.at[piece, flipped(me, have)]
        for bit in order[later:]:
            index = have | bit
            copies[piece, index] = copy_to(
                block,
                (block, {"dev": flipped(me, bit)}),
                send_sem.at[piece, index],
                recv_sem.at[piece, index],
            )

    for piece in range(pieces):
        out_ref[piece, me] = src_ref[piece]
    for piece in range(pieces):
        forward(piece, 0)
    for level in range(4):
        for piece in range(pieces):
            order = link_orders[piece]
            for have in subsets(order[:level]):
                copies[piece, have | order[level]].wait_recv()
                forward(piece, have | order[level])
            if both_groups and level == 2:
                for i in range(4):
                    far_copies[piece, i] = copy_to(
                        out_ref.at[piece, (1 - grp) * 8 + i * 2 + core],
                        (far_ref.at[piece, i * 2 + core], {"grp": 1 - grp}),
                        far_send.at[piece, i],
                        far_recv.at[piece, i],
                    )
    if both_groups:
        for piece in range(pieces):
            for i in range(4):
                far_copies[piece, i].wait_recv()
                block = far_ref.at[piece, i * 2 + core]
                near_copies[piece, i] = copy_to(
                    block,
                    (block, {"dev": flipped(me, 1)}),
                    far_send.at[piece, 4 + i],
                    far_recv.at[piece, 4 + i],
                )
        for copy in near_copies.values():
            copy.wait_recv()
    for group in (copies, far_copies, near_copies):
        for copy in group.values():
            copy.wait_send()


def spread(halves, both_groups, collective):
    pieces, part, block = halves.shape
    shapes = [jax.ShapeDtypeStruct((pieces, 16, part, block), halves.dtype)]
    scratch = [pltpu.SemaphoreType.DMA((pieces, 16)), pltpu.SemaphoreType.DMA((pieces, 16))]
    if both_groups:
        shapes.append(jax.ShapeDtypeStruct((pieces, 8, part, block), halves.dtype))
        scratch += [pltpu.SemaphoreType.DMA((pieces, 8)), pltpu.SemaphoreType.DMA((pieces, 8))]
    spec = pl.BlockSpec(memory_space=pltpu.VMEM)
    return pl.pallas_call(
        functools.partial(spread_kernel, both_groups),
        out_shape=tuple(shapes),
        in_specs=[spec],
        out_specs=tuple(spec for _ in shapes),
        scratch_shapes=scratch,
        compiler_params=pltpu.CompilerParams(
            collective_id=collective, has_side_effects=True, vmem_limit_bytes=16 * 2**20
        ),
    )(halves)


def moved_rows(
    stream,
    row_length,
    row_start,
    attn_gain,
    w_query,
    w_key,
    w_value,
    w_out,
    ffn_gain,
    w_gate,
    w_up,
    w_down,
):
    grp = lax.axis_index("grp")
    member = lax.axis_index("dev")
    members = lax.axis_size("dev")
    core, y, z_lo = member % 2, member // 2 % 2, member // 4 % 2
    slots, width = stream.shape
    half = width // 2
    part = slots // 2
    block = w_query.shape[1]
    kv_cols = w_key.shape[1]
    rows = slots // ROW_LEN
    blocks = half // block

    got = across(lax.dynamic_slice(stream, (core * part, (1 - grp) * half), (part, half)))
    sib = beside(got, 1)
    wide = stream.astype(jnp.float32)
    scale = lax.rsqrt(jnp.mean(wide * wide, axis=-1, keepdims=True) + 1e-05)
    far_scale = across(scale)
    half_gain = lax.dynamic_slice_in_dim(attn_gain, grp * half, half, 0)

    def scaled(rows_in, factor):
        return (rows_in.astype(jnp.float32) * factor * half_gain).astype(jnp.bfloat16)

    got = scaled(got, lax.dynamic_slice_in_dim(far_scale, core * part, part, 0))
    sib = scaled(sib, lax.dynamic_slice_in_dim(far_scale, (1 - core) * part, part, 0))
    near = scaled(lax.dynamic_slice_in_dim(stream, grp * half, half, 1), scale)
    w_all = jnp.concatenate([w_query, w_key, w_value], axis=1)
    back_got = across(dot(got, w_all))
    back_sib = across(dot(sib, w_all))
    own = dot(near, w_all)
    lo = jnp.where(core == 0, back_got, back_sib)
    hi = jnp.where(core == 0, back_sib, back_got)
    total = own + jnp.concatenate([lo, hi], axis=0)

    positions = (row_start[:, None] + jnp.arange(ROW_LEN, dtype=jnp.int32)[None, :]).reshape(-1)
    pair = (jnp.arange(HEAD_DIM, dtype=jnp.int32) // 2).astype(jnp.float32)
    freq = jnp.exp(-(2.0 * pair / HEAD_DIM) * math.log(rope_base))
    angle = positions.astype(jnp.float32)[:, None] * freq[None, :]
    cos, sin = jnp.cos(angle), jnp.sin(angle)
    heads = block // HEAD_DIM
    queries = turn(
        total[:, :block], jnp.tile(cos, (1, heads)), jnp.tile(sin, (1, heads))
    ).astype(jnp.bfloat16)
    key_first = core * kv_cols
    keys = turn(
        total[:, block : block + kv_cols],
        lax.dynamic_slice_in_dim(cos, key_first, kv_cols, 1),
        lax.dynamic_slice_in_dim(sin, key_first, kv_cols, 1),
    ).astype(jnp.bfloat16)
    values = total[:, block + kv_cols :].astype(jnp.bfloat16)

    mine = jnp.stack([keys, values])
    theirs = beside(mine, 1)
    both = jnp.where(
        core == 0,
        jnp.concatenate([mine, theirs], axis=2),
        jnp.concatenate([theirs, mine], axis=2),
    )
    qh = queries.reshape(rows, ROW_LEN, heads, HEAD_DIM)
    kh = both[0].reshape(rows, ROW_LEN, HEAD_DIM)
    vh = both[1].reshape(rows, ROW_LEN, HEAD_DIM)
    scores = jnp.einsum("rqhd,rjd->rhqj", qh, kh, preferred_element_type=jnp.float32) / math.sqrt(
        HEAD_DIM
    )
    at = jnp.arange(ROW_LEN, dtype=jnp.int32)
    allowed = (at[None, None, :] <= at[None, :, None]) & (
        at[None, None, :] < row_length[:, None, None]
    )
    scores = jnp.where(allowed[:, None], scores, -jnp.inf)
    top = jnp.max(scores, axis=-1, keepdims=True)
    expo = jnp.exp(scores - top)
    probs = (expo / jnp.sum(expo, axis=-1, keepdims=True)).astype(jnp.bfloat16)
    mixed = jnp.einsum("rhqj,rjd->rqhd", probs, vh, preferred_element_type=jnp.float32)
    mixed = mixed.astype(jnp.bfloat16).reshape(slots, block)

    z_hi = member // 8
    def by_blocks(blocked, weight):
        return lax.dot_general(
            blocked.reshape(blocks, part, block),
            weight.reshape(blocks, block, -1),
            (((0, 2), (0, 1)), ((), ())),
            preferred_element_type=jnp.float32,
        )

    w_out_far = across(after(w_out, back_got, back_sib))
    own_stream = lax.dynamic_slice_in_dim(stream, member * block, block, 1)
    gains = ffn_gain.reshape(2, blocks, 1, block)
    half_gain = pick(gains, grp, 0)
    (all_mixed,) = spread(mixed.reshape(2, part, block), False, 0)
    all_mixed = all_mixed.reshape(2, 2, blocks, part, block)
    attended = []
    for piece in range(2):
        span = slice(piece * part, (piece + 1) * part)
        projected = by_blocks(pick(all_mixed[piece], grp, 0), w_out) + by_blocks(
            pick(all_mixed[piece], 1 - grp, 0), w_out_far
        )
        attended.append((own_stream[span].astype(jnp.float32) + projected).astype(jnp.bfloat16))
    all_attended, far_rows_in = spread(jnp.stack(attended), True, 1)
    near_rows, far_rows = [], []
    wide = all_attended.astype(jnp.float32)
    mean = jnp.mean(jnp.mean(wide * wide, axis=3, keepdims=True), axis=1)
    scales = lax.rsqrt(mean + 1e-05)
    far_scales = across(scales)
    for piece in range(2):
        near = pick(all_attended[piece].reshape(2, blocks, part, block), grp, 0)
        near = near.astype(jnp.float32) * scales[piece] * half_gain
        far = far_rows_in[piece].astype(jnp.float32) * far_scales[piece] * half_gain
        near_rows.append(near.astype(jnp.bfloat16))
        far_rows.append(far.astype(jnp.bfloat16))
    far_attended = corner(after(jnp.concatenate(attended, axis=0), *far_rows))

    gate_far, up_far = [], []
    for far in far_rows:
        gate_far.append(across_sum(by_blocks(far, w_gate)))
        up_far.append(across_sum(by_blocks(far, w_up)))
    w_pairs = w_down.reshape(blocks // 2, 2, block, -1)
    w_send = pick(w_pairs, 1 - core, 1)
    w_keep = pick(w_pairs, core, 1)

    def down(rows_in, weight):
        return jnp.stack([dot_t(rows_in, weight[i]) for i in range(blocks // 2)])

    def summed_pairs(rows_in, piece):
        sums = down(rows_in, w_keep) + beside(down(rows_in, w_send), 1)
        sums = sums.reshape(2, 2, part, block)
        if piece == 0:
            return halve(halve(sums, 1, 2, y), 0, 4, z_lo)
        return halve(halve(sums, 0, 4, z_lo), 0, 2, y)

    is_near = z_hi == grp
    side = jnp.where(is_near, 0, 1)
    near_sums, far_sums = [], []
    for piece in range(2):
        gate = by_blocks(near_rows[piece], w_gate) + gate_far[piece]
        up = by_blocks(near_rows[piece], w_up) + up_far[piece]
        hidden = (jax.nn.silu(gate) * up).astype(jnp.bfloat16)
        far_hidden = across(hidden)
        near_sums.append(summed_pairs(hidden, piece))
        far_sums.append(summed_pairs(far_hidden, piece))
    done = []
    for piece in range(2):
        span = slice(piece * part, (piece + 1) * part)
        total = halve(jnp.stack([near_sums[piece], far_sums[piece]]), 0, 8, side)
        base = jnp.where(is_near, attended[piece], far_attended[span])
        ours = (base.astype(jnp.float32) + total).astype(jnp.bfloat16)
        done.append(jnp.where(is_near, ours, corner(ours)))
    return (keys, values, jnp.concatenate(done, axis=0))


def solution(mesh):
    exact = dict(mesh.shape) == {"grp": 2, "dev": 16}
    on_device = moved_rows if exact else gathered_weights
    placed = (
        P("grp", None),
        P("grp"),
        P("grp"),
        P(),
        P("grp", "dev"),
        P("grp", "dev"),
        P("grp", "dev"),
        P("grp", "dev"),
        P(),
        P("grp", "dev"),
        P("grp", "dev"),
        P("grp", "dev"),
    )
    return jax.shard_map(
        on_device,
        mesh=mesh,
        in_specs=placed,
        out_specs=(P("grp", "dev"), P("grp", "dev"), P("grp", "dev")),
        check_vma=False,
    )
```

```python
import functools
import math

import jax
import jax.numpy as jnp
from jax import lax
from jax.experimental import pallas as pl
from jax.experimental.pallas import tpu as pltpu
from jax.sharding import PartitionSpec as P

HEADS = 32
KV_HEADS = 8
HEAD_DIM = 128
ROW_LEN = 128


rope_base = 500000.0
wire = jnp.bfloat16


def norm_rows(values, gain):
    return values * lax.rsqrt(jnp.mean(values * values, axis=-1, keepdims=True) + 1e-05) * gain


def rotate(values, positions, first):
    cols = first + jnp.arange(values.shape[1], dtype=jnp.int32)
    pair = (cols % HEAD_DIM // 2).astype(jnp.float32)
    freq = jnp.exp(-(2.0 * pair / HEAD_DIM) * math.log(rope_base))
    angle = positions.astype(jnp.float32)[:, None] * freq[None, :]
    lead = values.reshape(values.shape[0], -1, 2)
    partner = jnp.stack([-lead[..., 1], lead[..., 0]], axis=-1).reshape(values.shape)
    return values * jnp.cos(angle) + partner * jnp.sin(angle)


def attend(queries, keys, values, offset, length):
    group = HEADS // KV_HEADS
    count = queries.shape[0]
    qh = queries.reshape(count, KV_HEADS, group, HEAD_DIM)
    kh = keys.reshape(-1, KV_HEADS, HEAD_DIM)
    vh = values.reshape(-1, KV_HEADS, HEAD_DIM)
    scores = jnp.einsum("qkgd,jkd->kgqj", qh, kh, preferred_element_type=jnp.float32) / math.sqrt(
        HEAD_DIM
    )
    query_pos = offset + jnp.arange(count, dtype=jnp.int32)
    key_pos = jnp.arange(keys.shape[0], dtype=jnp.int32)
    allowed = (key_pos[None, :] <= query_pos[:, None]) & (key_pos[None, :] < length)
    scores = jnp.where(allowed, scores, -jnp.inf)
    top = jnp.max(scores, axis=-1, keepdims=True)
    expo = jnp.exp(scores - top)
    probs = (expo / jnp.sum(expo, axis=-1, keepdims=True)).astype(jnp.bfloat16)
    mixed = jnp.einsum("kgqj,jkd->qkgd", probs, vh, preferred_element_type=jnp.float32)
    return mixed.astype(jnp.bfloat16).reshape(count, -1)


def gathered_weights(
    stream,
    row_length,
    row_start,
    attn_gain,
    w_query,
    w_key,
    w_value,
    w_out,
    ffn_gain,
    w_gate,
    w_up,
    w_down,
):
    member = lax.axis_index("dev")
    members = lax.axis_size("dev")
    w_query, w_key, w_value, w_out, w_gate, w_up, w_down = (
        lax.all_gather(w_query, "grp", axis=0, tiled=True),
        lax.all_gather(w_key, "grp", axis=0, tiled=True),
        lax.all_gather(w_value, "grp", axis=0, tiled=True),
        lax.all_gather(w_out, "grp", axis=0, tiled=True),
        lax.all_gather(w_gate, "grp", axis=0, tiled=True),
        lax.all_gather(w_up, "grp", axis=0, tiled=True),
        lax.all_gather(w_down, "grp", axis=0, tiled=True),
    )
    slots = stream.shape[0]
    query_cols = w_query.shape[1]
    kv_cols = w_key.shape[1]
    positions = (row_start[:, None] + jnp.arange(ROW_LEN, dtype=jnp.int32)[None, :]).reshape(-1)
    normed = norm_rows(stream.astype(jnp.float32), attn_gain).astype(jnp.bfloat16)
    queries = rotate(
        jnp.dot(normed, w_query, preferred_element_type=jnp.float32), positions, member * query_cols
    ).astype(jnp.bfloat16)
    keys = rotate(
        jnp.dot(normed, w_key, preferred_element_type=jnp.float32), positions, member * kv_cols
    ).astype(jnp.bfloat16)
    values = jnp.dot(normed, w_value, preferred_element_type=jnp.float32).astype(jnp.bfloat16)
    share = slots // members
    first = member * share
    all_queries, all_keys, all_values = (
        lax.all_gather(queries, "dev", axis=1, tiled=True),
        lax.all_gather(keys, "dev", axis=1, tiled=True),
        lax.all_gather(values, "dev", axis=1, tiled=True),
    )
    own_queries = lax.dynamic_slice_in_dim(all_queries, first, share, 0)
    row_index = first // ROW_LEN
    row_keys = lax.dynamic_slice_in_dim(all_keys, row_index * ROW_LEN, ROW_LEN, 0)
    row_values = lax.dynamic_slice_in_dim(all_values, row_index * ROW_LEN, ROW_LEN, 0)
    length = lax.dynamic_index_in_dim(row_length, row_index, 0, keepdims=False)
    mixed = attend(own_queries, row_keys, row_values, first - row_index * ROW_LEN, length)
    projected = jnp.dot(
        lax.all_gather(mixed, "dev", axis=0, tiled=True), w_out, preferred_element_type=jnp.float32
    )
    own_stream = lax.dynamic_slice_in_dim(stream, member * query_cols, query_cols, 1)
    attended = (own_stream.astype(jnp.float32) + projected).astype(jnp.bfloat16)
    full_rows = lax.all_gather(attended, "dev", axis=1, tiled=True)
    normed2 = norm_rows(full_rows.astype(jnp.float32), ffn_gain).astype(jnp.bfloat16)
    gate = jnp.dot(normed2, w_gate, preferred_element_type=jnp.float32)
    up = jnp.dot(normed2, w_up, preferred_element_type=jnp.float32)
    hidden = (jax.nn.silu(gate) * up).astype(jnp.bfloat16)
    partial_down = lax.dot_general(
        hidden, w_down, (((1,), (1,)), ((), ())), preferred_element_type=jnp.float32
    )
    summed = lax.psum_scatter(partial_down, "dev", scatter_dimension=1, tiled=True)
    next_stream = (attended.astype(jnp.float32) + summed).astype(jnp.bfloat16)
    return (keys, values, next_stream)


def across(values):
    return lax.ppermute(values, "grp", [(0, 1), (1, 0)])


def beside(values, bit):
    members = lax.axis_size("dev")
    return lax.ppermute(values, "dev", [(i, i ^ bit) for i in range(members)])


def corner(values):
    members = lax.axis_size("dev")
    top = members // 2
    pairs = []
    for grp in range(2):
        for dev in range(members):
            if dev // top != grp:
                pairs.append((grp * members + dev, (1 - grp) * members + (dev ^ top)))
    return lax.ppermute(values, ("grp", "dev"), pairs)


def pick(values, index, axis):
    return lax.dynamic_index_in_dim(values, index, axis, keepdims=False)


def after(values, *earlier):
    return lax.optimization_barrier((values,) + earlier)[0]


def turn(values, cos, sin):
    even = jnp.arange(values.shape[1], dtype=jnp.int32) % 2 == 0
    partner = jnp.where(even[None, :], -jnp.roll(values, -1, axis=1), jnp.roll(values, 1, axis=1))
    return values * cos + partner * sin


def halve(values, axis, bit, mine):
    away = pick(values, 1 - mine, axis).astype(wire)
    return pick(values, mine, axis) + beside(away, bit).astype(jnp.float32)


def across_sum(values):
    return across(values.astype(wire)).astype(jnp.float32)


def dot(a, b):
    return jnp.dot(a, b, preferred_element_type=jnp.float32)


def dot_t(a, b):
    return lax.dot_general(a, b, (((1,), (1,)), ((), ())), preferred_element_type=jnp.float32)


link_orders = ((8, 4, 2, 1), (2, 8, 4, 1))


def flipped(index, bits):
    for bit in (8, 4, 2, 1):
        if bits & bit:
            index = index + bit * (1 - 2 * (index // bit % 2))
    return index


def subsets(bits):
    found = [0]
    for bit in bits:
        found = found + [have | bit for have in found]
    return found


def spread_kernel(both_groups, src_ref, out_ref, *rest):
    if both_groups:
        far_ref, send_sem, recv_sem, far_send, far_recv = rest
    else:
        send_sem, recv_sem = rest
    grp, me = lax.axis_index("grp"), lax.axis_index("dev")
    core = me % 2
    barrier = pltpu.get_barrier_semaphore()
    targets = [{"dev": flipped(me, bit)} for bit in (8, 4, 2, 1)]
    if both_groups:
        targets.append({"grp": 1 - grp})
    for target in targets:
        pl.semaphore_signal(
            barrier, inc=1, device_id=target, device_id_type=pl.DeviceIdType.MESH
        )
    pl.semaphore_wait(barrier, len(targets))

    pieces = len(link_orders)
    copies, far_copies, near_copies = {}, {}, {}

    def copy_to(source, target, sent, arrived):
        copy = pltpu.make_async_remote_copy(
            src_ref=source,
            dst_ref=target[0],
            send_sem=sent,
            recv_sem=arrived,
            device_id=target[1],
            device_id_type=pl.DeviceIdType.MESH,
        )
        copy.start()
        return copy

    def forward(piece, have):
        order = link_orders[piece]
        later = 1 + max([order.index(bit) for bit in order if have & bit], default=-1)
        block = out_ref.at[piece, flipped(me, have)]
        for bit in order[later:]:
            index = have | bit
            copies[piece, index] = copy_to(
                block,
                (block, {"dev": flipped(me, bit)}),
                send_sem.at[piece, index],
                recv_sem.at[piece, index],
            )

    for piece in range(pieces):
        out_ref[piece, me] = src_ref[piece]
    for piece in range(pieces):
        forward(piece, 0)
    for level in range(4):
        for piece in range(pieces):
            order = link_orders[piece]
            for have in subsets(order[:level]):
                copies[piece, have | order[level]].wait_recv()
                forward(piece, have | order[level])
            if both_groups and level == 2:
                for i in range(4):
                    far_copies[piece, i] = copy_to(
                        out_ref.at[piece, (1 - grp) * 8 + i * 2 + core],
                        (far_ref.at[piece, i * 2 + core], {"grp": 1 - grp}),
                        far_send.at[piece, i],
                        far_recv.at[piece, i],
                    )
    if both_groups:
        for piece in range(pieces):
            for i in range(4):
                far_copies[piece, i].wait_recv()
                block = far_ref.at[piece, i * 2 + core]
                near_copies[piece, i] = copy_to(
                    block,
                    (block, {"dev": flipped(me, 1)}),
                    far_send.at[piece, 4 + i],
                    far_recv.at[piece, 4 + i],
                )
        for copy in near_copies.values():
            copy.wait_recv()
    for group in (copies, far_copies, near_copies):
        for copy in group.values():
            copy.wait_send()


def spread(halves, both_groups, collective):
    pieces, part, block = halves.shape
    shapes = [jax.ShapeDtypeStruct((pieces, 16, part, block), halves.dtype)]
    scratch = [pltpu.SemaphoreType.DMA((pieces, 16)), pltpu.SemaphoreType.DMA((pieces, 16))]
    if both_groups:
        shapes.append(jax.ShapeDtypeStruct((pieces, 8, part, block), halves.dtype))
        scratch += [pltpu.SemaphoreType.DMA((pieces, 8)), pltpu.SemaphoreType.DMA((pieces, 8))]
    spec = pl.BlockSpec(memory_space=pltpu.VMEM)
    return pl.pallas_call(
        functools.partial(spread_kernel, both_groups),
        out_shape=tuple(shapes),
        in_specs=[spec],
        out_specs=tuple(spec for _ in shapes),
        scratch_shapes=scratch,
        compiler_params=pltpu.CompilerParams(
            collective_id=collective, has_side_effects=True, vmem_limit_bytes=16 * 2**20
        ),
    )(halves)


def moved_rows(
    stream,
    row_length,
    row_start,
    attn_gain,
    w_query,
    w_key,
    w_value,
    w_out,
    ffn_gain,
    w_gate,
    w_up,
    w_down,
):
    grp = lax.axis_index("grp")
    member = lax.axis_index("dev")
    members = lax.axis_size("dev")
    core, y, z_lo = member % 2, member // 2 % 2, member // 4 % 2
    slots, width = stream.shape
    half = width // 2
    part = slots // 2
    block = w_query.shape[1]
    kv_cols = w_key.shape[1]
    rows = slots // ROW_LEN
    blocks = half // block

    got = across(lax.dynamic_slice(stream, (core * part, (1 - grp) * half), (part, half)))
    sib = beside(got, 1)
    wide = stream.astype(jnp.float32)
    scale = lax.rsqrt(jnp.mean(wide * wide, axis=-1, keepdims=True) + 1e-05)
    far_scale = across(scale)
    half_gain = lax.dynamic_slice_in_dim(attn_gain, grp * half, half, 0)

    def scaled(rows_in, factor):
        return (rows_in.astype(jnp.float32) * factor * half_gain).astype(jnp.bfloat16)

    got = scaled(got, lax.dynamic_slice_in_dim(far_scale, core * part, part, 0))
    sib = scaled(sib, lax.dynamic_slice_in_dim(far_scale, (1 - core) * part, part, 0))
    near = scaled(lax.dynamic_slice_in_dim(stream, grp * half, half, 1), scale)
    w_all = jnp.concatenate([w_query, w_key, w_value], axis=1)
    back_got = across(dot(got, w_all))
    back_sib = across(dot(sib, w_all))
    own = dot(near, w_all)
    lo = jnp.where(core == 0, back_got, back_sib)
    hi = jnp.where(core == 0, back_sib, back_got)
    total = own + jnp.concatenate([lo, hi], axis=0)

    positions = (row_start[:, None] + jnp.arange(ROW_LEN, dtype=jnp.int32)[None, :]).reshape(-1)
    pair = (jnp.arange(HEAD_DIM, dtype=jnp.int32) // 2).astype(jnp.float32)
    freq = jnp.exp(-(2.0 * pair / HEAD_DIM) * math.log(rope_base))
    angle = positions.astype(jnp.float32)[:, None] * freq[None, :]
    cos, sin = jnp.cos(angle), jnp.sin(angle)
    heads = block // HEAD_DIM
    queries = turn(
        total[:, :block], jnp.tile(cos, (1, heads)), jnp.tile(sin, (1, heads))
    ).astype(jnp.bfloat16)
    key_first = core * kv_cols
    keys = turn(
        total[:, block : block + kv_cols],
        lax.dynamic_slice_in_dim(cos, key_first, kv_cols, 1),
        lax.dynamic_slice_in_dim(sin, key_first, kv_cols, 1),
    ).astype(jnp.bfloat16)
    values = total[:, block + kv_cols :].astype(jnp.bfloat16)

    mine = jnp.stack([keys, values])
    theirs = beside(mine, 1)
    both = jnp.where(
        core == 0,
        jnp.concatenate([mine, theirs], axis=2),
        jnp.concatenate([theirs, mine], axis=2),
    )
    qh = queries.reshape(rows, ROW_LEN, heads, HEAD_DIM)
    kh = both[0].reshape(rows, ROW_LEN, HEAD_DIM)
    vh = both[1].reshape(rows, ROW_LEN, HEAD_DIM)
    scores = jnp.einsum("rqhd,rjd->rhqj", qh, kh, preferred_element_type=jnp.float32) / math.sqrt(
        HEAD_DIM
    )
    at = jnp.arange(ROW_LEN, dtype=jnp.int32)
    allowed = (at[None, None, :] <= at[None, :, None]) & (
        at[None, None, :] < row_length[:, None, None]
    )
    scores = jnp.where(allowed[:, None], scores, -jnp.inf)
    top = jnp.max(scores, axis=-1, keepdims=True)
    expo = jnp.exp(scores - top)
    probs = (expo / jnp.sum(expo, axis=-1, keepdims=True)).astype(jnp.bfloat16)
    mixed = jnp.einsum("rhqj,rjd->rqhd", probs, vh, preferred_element_type=jnp.float32)
    mixed = mixed.astype(jnp.bfloat16).reshape(slots, block)

    z_hi = member // 8
    def by_blocks(blocked, weight):
        return lax.dot_general(
            blocked.reshape(blocks, part, block),
            weight.reshape(blocks, block, -1),
            (((0, 2), (0, 1)), ((), ())),
            preferred_element_type=jnp.float32,
        )

    w_out_far = across(after(w_out, back_got, back_sib))
    own_stream = lax.dynamic_slice_in_dim(stream, member * block, block, 1)
    gains = ffn_gain.reshape(2, blocks, 1, block)
    half_gain = pick(gains, grp, 0)
    (all_mixed,) = spread(mixed.reshape(2, part, block), False, 0)
    all_mixed = all_mixed.reshape(2, 2, blocks, part, block)
    attended = []
    for piece in range(2):
        span = slice(piece * part, (piece + 1) * part)
        projected = by_blocks(pick(all_mixed[piece], grp, 0), w_out) + by_blocks(
            pick(all_mixed[piece], 1 - grp, 0), w_out_far
        )
        attended.append((own_stream[span].astype(jnp.float32) + projected).astype(jnp.bfloat16))
    all_attended, far_rows_in = spread(jnp.stack(attended), True, 1)
    near_rows, far_rows = [], []
    wide = all_attended.astype(jnp.float32)
    mean = jnp.mean(jnp.mean(wide * wide, axis=3, keepdims=True), axis=1)
    scales = lax.rsqrt(mean + 1e-05)
    far_scales = across(scales)
    for piece in range(2):
        near = pick(all_attended[piece].reshape(2, blocks, part, block), grp, 0)
        near = near.astype(jnp.float32) * scales[piece] * half_gain
        far = far_rows_in[piece].astype(jnp.float32) * far_scales[piece] * half_gain
        near_rows.append(near.astype(jnp.bfloat16))
        far_rows.append(far.astype(jnp.bfloat16))
    far_attended = corner(after(jnp.concatenate(attended, axis=0), *far_rows))

    gate_far, up_far = [], []
    for far in far_rows:
        gate_far.append(across_sum(by_blocks(far, w_gate)))
        up_far.append(across_sum(by_blocks(far, w_up)))
    w_pairs = w_down.reshape(blocks // 2, 2, block, -1)
    w_send = pick(w_pairs, 1 - core, 1)
    w_keep = pick(w_pairs, core, 1)

    def down(rows_in, weight):
        return jnp.stack([dot_t(rows_in, weight[i]) for i in range(blocks // 2)])

    def summed_pairs(rows_in, piece):
        sums = down(rows_in, w_keep) + beside(down(rows_in, w_send), 1)
        sums = sums.reshape(2, 2, part, block)
        if piece == 0:
            return halve(halve(sums, 1, 2, y), 0, 4, z_lo)
        return halve(halve(sums, 0, 4, z_lo), 0, 2, y)

    is_near = z_hi == grp
    side = jnp.where(is_near, 0, 1)
    near_sums, far_sums = [], []
    for piece in range(2):
        gate = by_blocks(near_rows[piece], w_gate) + gate_far[piece]
        up = by_blocks(near_rows[piece], w_up) + up_far[piece]
        hidden = (jax.nn.silu(gate) * up).astype(jnp.bfloat16)
        far_hidden = across(hidden)
        near_sums.append(summed_pairs(hidden, piece))
        far_sums.append(summed_pairs(far_hidden, piece))
    done = []
    for piece in range(2):
        span = slice(piece * part, (piece + 1) * part)
        total = halve(jnp.stack([near_sums[piece], far_sums[piece]]), 0, 8, side)
        base = jnp.where(is_near, attended[piece], far_attended[span])
        ours = (base.astype(jnp.float32) + total).astype(jnp.bfloat16)
        done.append(jnp.where(is_near, ours, corner(ours)))
    return (keys, values, jnp.concatenate(done, axis=0))


def solution(mesh):
    exact = dict(mesh.shape) == {"grp": 2, "dev": 16}
    on_device = moved_rows if exact else gathered_weights
    placed = (
        P("grp", None),
        P("grp"),
        P("grp"),
        P(),
        P("grp", "dev"),
        P("grp", "dev"),
        P("grp", "dev"),
        P("grp", "dev"),
        P(),
        P("grp", "dev"),
        P("grp", "dev"),
        P("grp", "dev"),
    )
    return jax.shard_map(
        on_device,
        mesh=mesh,
        in_specs=placed,
        out_specs=(P("grp", "dev"), P("grp", "dev"), P("grp", "dev")),
        check_vma=False,
    )
```
